512 devices in a mesh: dp: 64 (over y, x, z_lo), tensor: 8 (over z_hi, core).
Axes of the slice: x: 4, y: 8, z: 8 (z_hi: 4, z_lo: 2; z = z_hi * 2 + z_lo), core: 2. Of those that a mesh axis runs over, the one named last changes fastest.
Arguments:
- activations: bfloat16 [128000, 512], P('dp'), may hold values from -26 to 26
- out_grad: bfloat16 [128000, 8192], P('dp', 'tensor'), may hold values from -0.07267221 to 0.07267221
- weight: float32 [512, 8192], P('dp', 'tensor'), may hold values from -0.25 to 0.25
- row_moment: float32 [512], P('dp'), may hold values from 0.08 to 1.24
- col_moment: float32 [8192], P('tensor'), may hold values from 0.1 to 1
Outputs:
- new_weight: float32 [512, 8192], P('dp', 'tensor')
- step_taken: float32 [512, 8192], P('dp', 'tensor')
- row_next: float32 [512], P('dp')
- col_next: float32 [8192], P('tensor')
- row_factor: float32 [512], P('dp')
The draws below stay inside these ranges and needn't reach their ends.
All inputs are finite; a program needn't handle non-finite values.
Results may differ from the reference program's by a relative error of at most 0.0003.
Values sent between devices are 32-bit elements; how exact they have to be, the bound alone decides.
No kernel may reach another device: no remote copies, remote signals or barrier semaphores. Data moves between devices by JAX's collectives and lax.ppermute only.
A program may use at most 64 MiB of HBM per device.

```python
import math
import jax
import jax.numpy as jnp
from jax import lax

D = 8192
ROWS = 512
TOKENS = 128000


def scaled_field(key, rows, cols, rise):
    base_key, rough_key = jax.random.split(key)
    place = jnp.arange(cols).astype(jnp.float32) / max(cols - 1, 1)
    rough = jnp.exp(jax.random.uniform(rough_key, (cols,), jnp.float32, -0.35, 0.35))
    column_scale = jnp.exp(jnp.log(rise) * place) * rough
    values = jnp.clip(jax.random.normal(base_key, (rows, cols), jnp.float32), -3.0, 3.0)
    return values * column_scale[None, :]


def draw_activations(key, part):
    key = jax.random.fold_in(key, 11)
    values = scaled_field(key, TOKENS, ROWS, 3.0)
    return values.astype(jnp.bfloat16)


def draw_out_grad(key, part):
    key = jax.random.fold_in(key, 13)
    values = scaled_field(key, TOKENS, D, 3.0)
    return (values * TOKENS ** (-0.5)).astype(jnp.bfloat16)


def draw_row_moment(key, part):
    key = jax.random.fold_in(key, 7)
    place = jnp.arange(ROWS).astype(jnp.float32) / max(ROWS - 1, 1)
    noise = jnp.clip(0.35 * jax.random.normal(key, (ROWS,), jnp.float32), -0.7, 0.7)
    return (0.2 * jnp.exp(noise) * (1.0 + 2.0 * place)).astype(jnp.float32)


def levels(stream_key, dims, pieces, smallest, largest):
    def one(position, parts):
        steps = jax.random.uniform(jax.random.fold_in(jax.random.fold_in(stream_key, 6), position), (parts,), jnp.float32, smallest / len(pieces), largest / len(pieces))
        return jnp.repeat(jnp.exp(steps), dims[position] // parts).reshape((-1,) + (1,) * (len(dims) - position - 1))

    level = one(*pieces[0])
    for cut in pieces[1:]:
        level = level * one(*cut)
    return level


def bell_draw(key, shape, deviation, limit, cuts=(), dtype=jnp.bfloat16):
    factor_of = levels(key, shape, cuts, -0.22, 0.18) if cuts else 1.0
    result = jax.random.normal(key, shape, jnp.float32) * deviation * factor_of
    return jnp.minimum(jnp.maximum(result, -limit), limit).astype(dtype)


def setup_inputs(seed: int = 0) -> dict:
    arg_keys = jax.random.split(jax.random.key(seed), 6)
    activations = draw_activations(jax.random.fold_in(arg_keys[5], 71), 0)
    out_grad = draw_out_grad(jax.random.fold_in(arg_keys[5], 71), 0)
    weight = bell_draw(arg_keys[2], (ROWS, D), ROWS ** -0.5, 0.25, ((0, 64), (1, 8)), jnp.float32)
    row_moment = draw_row_moment(jax.random.fold_in(arg_keys[5], 71), 0)
    col_moment = jnp.clip(jnp.exp(math.log(1.0) - 2.3025851 * jax.random.uniform(arg_keys[4], (D,), jnp.float32) ** levels(arg_keys[4], (D,), ((0, 8),), -0.2, 0.2)), 0.1, 1.0)
    return dict(activations=activations, out_grad=out_grad, weight=weight, row_moment=row_moment, col_moment=col_moment)


tiny_square = 1e-30
decay_rate = 0.8
clip_level = 0.25
learn_rate = 0.01

def reference(activations, out_grad, weight, row_moment, col_moment):
    grad = jnp.dot(activations.T, out_grad, preferred_element_type=jnp.float32)
    squares = grad * grad + tiny_square
    row_next = decay_rate * row_moment + (1.0 - decay_rate) * lax.optimization_barrier(jnp.mean(squares, axis=1))
    col_next = decay_rate * col_moment + (1.0 - decay_rate) * lax.optimization_barrier(jnp.mean(squares, axis=0))
    row_mean = jnp.mean(row_next)
    row_factor = row_next / row_mean
    scaled = grad / jnp.sqrt(row_next[:, None] * col_next[None, :] / row_mean)
    rms = jnp.sqrt(jnp.mean(scaled * scaled))
    step_taken = scaled / jnp.maximum(1.0, rms / clip_level)
    return (weight - learn_rate * step_taken, step_taken, row_next, col_next, row_factor)
```

```python
import jax
import jax.numpy as jnp
from jax import lax
from jax.sharding import PartitionSpec as P

tiny_square = 1e-30
decay_rate = 0.8
clip_level = 0.25
learn_rate = 0.01


def shared_sum(values, axis):
    members = lax.axis_size(axis)
    copies = jnp.broadcast_to(values[None], (members,) + values.shape)
    return jnp.sum(lax.all_to_all(copies, axis, 0, 0), axis=0)


def body(activations, out_grad, weight, row_moment, col_moment):
    own_rows = weight.shape[0]
    own_cols = weight.shape[1]
    owners = lax.axis_size("dp")
    all_rows = own_rows * owners
    all_cols = own_cols * lax.axis_size("tensor")
    partial = lax.dot_general(
        activations, out_grad, (((0,), (0,)), ((), ())), preferred_element_type=jnp.float32
    )
    pieces = lax.all_to_all(partial.reshape(owners, own_rows, own_cols), "dp", 0, 0)
    grad = jnp.sum(pieces, axis=0)
    squares = grad * grad + tiny_square
    col_sq = shared_sum(jnp.sum(squares, axis=0).reshape(-1, 128), "dp").reshape(own_cols)
    col_next = decay_rate * col_moment + (1.0 - decay_rate) * col_sq / all_rows
    row_sq = jnp.sum(squares, axis=1)
    row_scaled = jnp.sum(grad * grad / col_next[None, :], axis=1)
    rows = shared_sum(jnp.stack([row_sq, row_scaled]), "tensor")
    row_next = decay_rate * row_moment + (1.0 - decay_rate) * rows[0] / all_cols
    totals = shared_sum(jnp.stack([jnp.sum(row_next), jnp.sum(rows[1] / row_next)])[None], "dp")[0]
    row_mean = totals[0] / all_rows
    row_factor = row_next / row_mean
    rms = jnp.sqrt(totals[1] * row_mean / (all_rows * all_cols))
    scaled = grad / jnp.sqrt(row_next[:, None] * col_next[None, :] / row_mean)
    step_taken = scaled / jnp.maximum(1.0, rms / clip_level)
    return (weight - learn_rate * step_taken, step_taken, row_next, col_next, row_factor)


def solution(mesh):
    return jax.shard_map(
        body,
        mesh=mesh,
        in_specs=(P("dp", None), P("dp", "tensor"), P("dp", "tensor"), P("dp"), P("tensor")),
        out_specs=(P("dp", "tensor"), P("dp", "tensor"), P("dp"), P("tensor"), P("dp")),
        check_vma=False,
    )
```

```python
import functools

import jax
import jax.numpy as jnp
from jax import lax
from jax.experimental import pallas as pl
from jax.experimental.pallas import tpu as pltpu
from jax.sharding import Mesh
from jax.sharding import PartitionSpec as P

tiny_square = 1e-30
decay_rate = 0.8
clip_level = 0.25
learn_rate = 0.01

FIRST = ("y_lo", "x", "z_lo")
SECOND = ("y_hi",)
DP = ("y_hi", "y_lo", "x", "z_lo")
TENSOR = ("z_hi", "core")
SIZES = (4, 2, 4, 2, 4, 2)
LANES = 128
MIB = 2**20

VMEM = pl.BlockSpec(memory_space=pltpu.VMEM)
SMEM = pl.BlockSpec(memory_space=pltpu.SMEM)


def product_kernel(outer, middle, act_ref, cot_ref, out_ref):
    value = lax.dot_general(
        act_ref[...], cot_ref[...], (((0,), (0,)), ((), ())), preferred_element_type=jnp.float32
    )
    run = out_ref.shape[1] // outer
    for o in range(outer):
        for m in range(middle):
            at = (o * middle + m) * run
            out_ref[m, o * run : (o + 1) * run, :] = value[at : at + run, :]


def product(activations, out_grad, outer, middle):
    tokens, rows = activations.shape
    cols = out_grad.shape[1]
    width = 256
    return pl.pallas_call(
        functools.partial(product_kernel, outer, middle),
        grid=(cols // width,),
        in_specs=[
            pl.BlockSpec((tokens, rows), lambda j: (0, 0)),
            pl.BlockSpec((tokens, width), lambda j: (0, j)),
        ],
        out_specs=pl.BlockSpec((middle, rows // middle, width), lambda j: (0, 0, j)),
        out_shape=jax.ShapeDtypeStruct((middle, rows // middle, cols), jnp.float32),
        compiler_params=pltpu.CompilerParams(vmem_limit_bytes=56 * MIB),
        name="product",
    )(activations, out_grad)


def split_kernel(pieces_ref, out_ref):
    owners, _, rows, width = out_ref.shape
    own = rows // owners
    for c in range(owners):
        at = slice(c * width, (c + 1) * width)
        block = jnp.sum(pieces_ref[:, :, at], axis=0)
        out_ref[c, 0] = block
        for owner in range(owners):
            out_ref[owner, 1, c * own : (c + 1) * own, :] = block[owner * own : (owner + 1) * own]


def column_kernel(pieces_ref, grad_ref, own_ref, copies_ref):
    grad = jnp.sum(pieces_ref[:, 0], axis=0)
    grad_ref[...] = grad
    own_ref[...] = jnp.sum(pieces_ref[:, 1], axis=0)
    sums = jnp.sum(grad * grad + tiny_square, axis=0, keepdims=True)
    copies_ref[...] = jnp.broadcast_to(sums[None], copies_ref.shape)


def row_kernel(all_rows, all_cols, each, place_ref, row_moment_ref, cols_ref, col_moment_ref, grad_ref, message_ref):
    place = place_ref[0]
    col_next = (
        decay_rate * col_moment_ref[place] + (1.0 - decay_rate) * jnp.sum(cols_ref[...], axis=0) / all_rows
    )
    grad = grad_ref[...]
    square = grad * grad
    both = jnp.concatenate([square + tiny_square, square / col_next], axis=0)
    width = both.shape[1]
    both = sum(both[:, at : at + LANES] for at in range(0, width, LANES))
    both = jnp.concatenate([both, jnp.zeros((LANES - both.shape[0], LANES), jnp.float32)], axis=0)
    sums = jnp.sum(both.T, axis=0, keepdims=True)
    lane = lax.broadcasted_iota(jnp.int32, sums.shape, 1)
    scale = decay_rate / (1.0 - decay_rate) * all_cols / each
    own = row_moment_ref.shape[0]
    for r in range(own):
        sums = sums + jnp.where(lane == place * own + r, scale * row_moment_ref[r], 0.0)
    parts = [sums] + [col_next[:, at : at + LANES] for at in range(0, width, LANES)]
    parts += [jnp.zeros((message_ref.shape[1] - len(parts), LANES), jnp.float32)]
    message_ref[...] = jnp.broadcast_to(jnp.concatenate(parts, axis=0)[None], message_ref.shape)


def to_lanes(column):
    n = column.shape[0]
    here = lax.broadcasted_iota(jnp.int32, (n, LANES), 0) == lax.broadcasted_iota(jnp.int32, (n, LANES), 1)
    return jnp.sum(jnp.where(here, jnp.broadcast_to(column, (n, LANES)), 0.0), axis=0)[:n]


def update_kernel(all_cols, place_ref, message_ref, own_ref, update_ref, row_ref, col_ref, rows_ref, copies_ref):
    place, mine = place_ref[0], place_ref[1]
    owners, _, width = col_ref.shape
    rows = own_ref.shape[0]
    own, each = rows // owners, message_ref.shape[0] // owners
    sums = jnp.sum(message_ref[:, 0], axis=0, keepdims=True)
    row_next = (1.0 - decay_rate) / all_cols * sums[:, :rows]
    total = jnp.sum(sums[:, rows : 2 * rows] / row_next, axis=1, keepdims=True)
    row_sum = jnp.sum(row_next, axis=1, keepdims=True)
    lane = lax.broadcasted_iota(jnp.int32, (1, LANES), 1)
    copies_ref[...] = jnp.broadcast_to(jnp.where(lane < LANES // 2, total, row_sum)[None], copies_ref.shape)
    wide = jnp.broadcast_to(row_next, (own, rows))
    lane = lax.broadcasted_iota(jnp.int32, (own, rows), 1)
    here = lax.broadcasted_iota(jnp.int32, (own, rows), 0) + place * own
    column = jnp.sum(jnp.where(lane == here, wide, 0.0), axis=1, keepdims=True)
    row_ref[...] = to_lanes(column)
    rows_ref[...] = jnp.broadcast_to(column, rows_ref.shape)
    for owner in range(owners):
        source = owner * each + mine
        parts = [message_ref[source, k + 1 : k + 2] for k in range(width // LANES)]
        col_next = jnp.concatenate(parts, axis=1)
        col_ref[owner] = col_next
        grad = own_ref[owner * own : (owner + 1) * own]
        update_ref[:, owner * width : (owner + 1) * width] = grad / jnp.sqrt(column * col_next)


def finish_kernel(all_rows, all_cols, sums_ref, update_ref, rows_ref, weight_ref, new_ref, step_ref, factor_ref):
    sums = jnp.sum(sums_ref[...], axis=0)
    total, row_mean = sums[:, 0:1], sums[:, LANES - 1 :] / all_rows
    rms = jnp.sqrt(total * row_mean / (all_rows * all_cols))
    step = update_ref[...] * (jnp.sqrt(row_mean) / jnp.maximum(1.0, rms / clip_level))
    step_ref[...] = step
    new_ref[...] = weight_ref[...] - learn_rate * step
    factor_ref[...] = to_lanes(rows_ref[:, 0:1] / row_mean)


def call(kernel, outs, ins, name):
    return pl.pallas_call(
        kernel,
        in_specs=ins,
        out_specs=[VMEM] * len(outs),
        out_shape=[jax.ShapeDtypeStruct(shape, jnp.float32) for shape in outs],
        compiler_params=pltpu.CompilerParams(vmem_limit_bytes=32 * MIB),
        name=name,
    )


def body(activations, out_grad, weight, row_moment, col_moment):
    own_rows, own_cols = weight.shape
    all_rows = own_rows * lax.axis_size(DP)
    all_cols = own_cols * lax.axis_size(TENSOR)
    first, second, tensor = lax.axis_size(FIRST), lax.axis_size(SECOND), lax.axis_size(TENSOR)
    rows, width = second * own_rows, own_cols // second
    place = jnp.stack([lax.axis_index(SECOND), lax.axis_index(TENSOR)]).astype(jnp.int32)

    partial = product(activations, out_grad, lax.axis_size(SECOND), first)
    pieces = lax.all_to_all(partial, FIRST, 0, 0)
    (pieces,) = call(split_kernel, [(second, 2, rows, width)], [VMEM], "split")(pieces)
    pieces = lax.all_to_all(pieces, SECOND, 0, 0)
    grad, own, copies = call(
        column_kernel, [(rows, width), (rows, width), (first, 1, width)], [VMEM], "columns"
    )(pieces)
    cols = lax.all_to_all(copies, FIRST, 0, 0)
    (message,) = call(
        functools.partial(row_kernel, all_rows, all_cols, tensor),
        [(second * tensor, 4, LANES)],
        [SMEM, SMEM, VMEM, VMEM, VMEM],
        "rows",
    )(place, row_moment, cols, col_moment.reshape(second, 1, width), grad)
    message = lax.all_to_all(message, SECOND + TENSOR, 0, 0)
    update, row_next, col_next, rows_wide, copies = call(
        functools.partial(update_kernel, all_cols),
        [(own_rows, own_cols), (own_rows,), (second, 1, width), (own_rows, LANES), (first, 1, LANES)],
        [SMEM, VMEM, VMEM],
        "update",
    )(place, message, own)
    sums = lax.all_to_all(copies, FIRST, 0, 0)
    new_weight, step_taken, row_factor = call(
        functools.partial(finish_kernel, all_rows, all_cols),
        [(own_rows, own_cols), (own_rows, own_cols), (own_rows,)],
        [VMEM] * 4,
        "finish",
    )(sums, update, rows_wide, weight)
    return new_weight, step_taken, row_next, col_next.reshape(own_cols), row_factor


def solution(mesh):
    physical = Mesh(mesh.devices.reshape(SIZES), DP + TENSOR)
    return jax.shard_map(
        body,
        mesh=physical,
        in_specs=(P(DP, None), P(DP, TENSOR), P(DP, TENSOR), P(DP), P(TENSOR)),
        out_specs=(P(DP, TENSOR), P(DP, TENSOR), P(DP), P(TENSOR), P(DP)),
        check_vma=False,
    )
```

```python
import functools

import jax
import jax.numpy as jnp
import numpy as np
from jax import lax
from jax.experimental import pallas as pl
from jax.experimental.pallas import tpu as pltpu
from jax.sharding import Mesh
from jax.sharding import PartitionSpec as P

tiny_square = 1e-30
decay_rate = 0.8
clip_level = 0.25
learn_rate = 0.01

FIRST = ("z_lo", "x", "y_lo")
SECOND = ("y_hi",)
DP = ("y_hi", "y_lo", "x", "z_lo")
TENSOR = ("z_hi", "core")
SIZES = (4, 2, 4, 2, 4, 2)
LANES = 128
MIB = 2**20

VMEM = pl.BlockSpec(memory_space=pltpu.VMEM)
SMEM = pl.BlockSpec(memory_space=pltpu.SMEM)


def product_kernel(chunk, act_hbm, cot_hbm, out_ref, act, cot, total, act_sems, cot_sems):
    tokens, cols = cot.shape
    members, block, _ = out_ref.shape
    owners, run = lax.axis_size(SECOND), block // lax.axis_size(SECOND)
    parts = [pl.ds(at, min(chunk, tokens - at)) for at in range(0, tokens, chunk)]
    copies = []
    for i, part in enumerate(parts):
        pair = (
            pltpu.make_async_copy(act_hbm.at[part], act.at[part], act_sems.at[i]),
            pltpu.make_async_copy(cot_hbm.at[part], cot.at[part], cot_sems.at[i]),
        )
        for copy in pair:
            copy.start()
        copies.append(pair)
    for i, part in enumerate(parts):
        for copy in copies[i]:
            copy.wait()
        value = jnp.dot(act[part].T, cot[part], preferred_element_type=jnp.float32)
        if i > 0:
            value = total[...] + value
        if i < len(parts) - 1:
            total[...] = value
    order = np.arange(members).reshape([lax.axis_size(name) for name in DP[1:]])
    order = order.transpose([DP[1:].index(name) for name in FIRST]).reshape(-1)
    for owner in range(owners):
        for member in range(members):
            at = (owner * members + int(order[member])) * run
            out_ref[member, owner * run : (owner + 1) * run, :] = value[at : at + run, :]


def product(activations, out_grad, members):
    tokens, rows = activations.shape
    cols = out_grad.shape[1]
    chunk = 512
    n = pl.cdiv(tokens, chunk)
    return pl.pallas_call(
        functools.partial(product_kernel, chunk),
        in_specs=[pl.BlockSpec(memory_space=pl.ANY)] * 2,
        out_specs=VMEM,
        out_shape=jax.ShapeDtypeStruct((members, rows // members, cols), jnp.float32),
        scratch_shapes=[
            pltpu.VMEM((tokens, rows), activations.dtype),
            pltpu.VMEM((tokens, cols), out_grad.dtype),
            pltpu.VMEM((rows, cols), jnp.float32),
            pltpu.SemaphoreType.DMA((n,)),
            pltpu.SemaphoreType.DMA((n,)),
        ],
        compiler_params=pltpu.CompilerParams(vmem_limit_bytes=56 * MIB),
        name="product",
    )(activations, out_grad)


def split_kernel(place_ref, row_moment_ref, pieces_ref, out_ref):
    place, own = place_ref[0], row_moment_ref.shape[0]
    cols = pieces_ref.shape[2]
    for at in range(0, cols, LANES):
        block = jnp.sum(pieces_ref[:, :, at : at + LANES], axis=0)
        out_ref[:, :, at : at + LANES] = jnp.broadcast_to(block[None], (out_ref.shape[0],) + block.shape)
    lane = lax.broadcasted_iota(jnp.int32, block.shape, 1)
    moments = jnp.zeros(block.shape, jnp.float32)
    for r in range(own):
        moments = jnp.where(lane == place * own + r, row_moment_ref[r], moments)
    out_ref[:, :, cols:] = jnp.broadcast_to(moments[None], (out_ref.shape[0],) + block.shape)


def column_kernel(pieces_ref, grad_ref, moment_ref, copies_ref):
    cols = grad_ref.shape[1]
    grad = jnp.sum(pieces_ref[:, :, :cols], axis=0)
    grad_ref[...] = grad
    moment_ref[...] = jnp.sum(pieces_ref[:, :1, cols:], axis=0)
    sums = jnp.sum(grad * grad + tiny_square, axis=0, keepdims=True)
    copies_ref[...] = jnp.broadcast_to(sums[None], copies_ref.shape)


def row_kernel(all_rows, all_cols, each, cols_ref, col_moment_ref, grad_ref, moment_ref, col_ref, message_ref):
    col_next = (
        decay_rate * col_moment_ref[...] + (1.0 - decay_rate) * jnp.sum(cols_ref[...], axis=0) / all_rows
    )
    col_ref[...] = col_next
    grad = grad_ref[...]
    rows, cols = grad.shape
    square = grad * grad
    both = jnp.concatenate([square + tiny_square, square / col_next], axis=0)
    both = sum(both[:, at : at + LANES] for at in range(0, cols, LANES))
    both = jnp.concatenate([both, jnp.zeros((LANES - 2 * rows, LANES), jnp.float32)], axis=0)
    sums = jnp.sum(both.T, axis=0, keepdims=True)
    sums = sums + (decay_rate / (1.0 - decay_rate) * all_cols / each) * moment_ref[...]
    message_ref[...] = jnp.broadcast_to(sums[None], message_ref.shape)


def to_lanes(column):
    n = column.shape[0]
    here = lax.broadcasted_iota(jnp.int32, (n, LANES), 0) == lax.broadcasted_iota(jnp.int32, (n, LANES), 1)
    return jnp.sum(jnp.where(here, jnp.broadcast_to(column, (n, LANES)), 0.0), axis=0)[:n]


def finish_kernel(
    all_rows, all_cols, place_ref, message_ref, col_ref, grad_ref, weight_ref, new_ref, step_ref, row_ref, factor_ref
):
    place, member = place_ref[0], place_ref[1]
    own, rows = weight_ref.shape[0], grad_ref.shape[0]
    blocks = all_rows // rows
    each = message_ref.shape[0] // blocks
    sums = jnp.sum(message_ref[:, 0].reshape(blocks, each, LANES), axis=1)
    row_next = (1.0 - decay_rate) / all_cols * sums[:, :rows]
    scaled = sums[:, rows : 2 * rows] / row_next
    total = jnp.sum(jnp.sum(scaled, axis=1, keepdims=True), axis=0, keepdims=True)
    row_mean = jnp.sum(jnp.sum(row_next, axis=1, keepdims=True), axis=0, keepdims=True) / all_rows
    mine = lax.broadcasted_iota(jnp.int32, row_next.shape, 0) == member
    row_next = jnp.sum(jnp.where(mine, row_next, 0.0), axis=0, keepdims=True)
    lane = lax.broadcasted_iota(jnp.int32, (own, rows), 1)
    here = lax.broadcasted_iota(jnp.int32, (own, rows), 0) + place * own
    column = jnp.sum(jnp.where(lane == here, jnp.broadcast_to(row_next, (own, rows)), 0.0), axis=1, keepdims=True)
    row_ref[...] = to_lanes(column)
    factor_ref[...] = to_lanes(column / row_mean)
    rms = jnp.sqrt(total * row_mean / (all_rows * all_cols))
    grad = grad_ref[pl.ds(pl.multiple_of(place * own, own), own), :]
    scaled = grad / jnp.sqrt(column * col_ref[...] / row_mean)
    step = scaled / jnp.maximum(1.0, rms / clip_level)
    step_ref[...] = step
    new_ref[...] = weight_ref[...] - learn_rate * step


def call(kernel, outs, ins, name):
    return pl.pallas_call(
        kernel,
        in_specs=ins,
        out_specs=[VMEM] * len(outs),
        out_shape=[jax.ShapeDtypeStruct(shape, jnp.float32) for shape in outs],
        compiler_params=pltpu.CompilerParams(vmem_limit_bytes=32 * MIB),
        name=name,
    )


def body(activations, out_grad, weight, row_moment, col_moment):
    own_rows, cols = weight.shape
    all_rows = own_rows * lax.axis_size(DP)
    all_cols = cols * lax.axis_size(TENSOR)
    first, second, tensor = lax.axis_size(FIRST), lax.axis_size(SECOND), lax.axis_size(TENSOR)
    rows = second * own_rows
    place = jnp.stack([lax.axis_index(SECOND), lax.axis_index(FIRST)]).astype(jnp.int32)

    pieces = lax.all_to_all(product(activations, out_grad, first), FIRST, 0, 0)
    (pieces,) = call(split_kernel, [(second, rows, cols + LANES)], [SMEM, SMEM, VMEM], "split")(
        place, row_moment, pieces
    )
    pieces = lax.all_to_all(pieces, SECOND, 0, 0)
    grad, moment, copies = call(
        column_kernel, [(rows, cols), (1, LANES), (first, 1, cols)], [VMEM], "columns"
    )(pieces)
    copies = lax.all_to_all(copies, FIRST, 0, 0)
    col_next, message = call(
        functools.partial(row_kernel, all_rows, all_cols, tensor),
        [(1, cols), (first * tensor, 1, LANES)],
        [VMEM] * 4,
        "rows",
    )(copies, col_moment.reshape(1, cols), grad, moment)
    message = lax.all_to_all(message, FIRST + TENSOR, 0, 0)
    new_weight, step_taken, row_next, row_factor = call(
        functools.partial(finish_kernel, all_rows, all_cols),
        [(own_rows, cols), (own_rows, cols), (own_rows,), (own_rows,)],
        [SMEM] + [VMEM] * 4,
        "finish",
    )(place, message, col_next, grad, weight)
    return new_weight, step_taken, row_next, col_next.reshape(cols), row_factor


def solution(mesh):
    physical = Mesh(mesh.devices.reshape(SIZES), DP + TENSOR)
    return jax.shard_map(
        body,
        mesh=physical,
        in_specs=(P(DP, None), P(DP, TENSOR), P(DP, TENSOR), P(DP), P(TENSOR)),
        out_specs=(P(DP, TENSOR), P(DP, TENSOR), P(DP), P(TENSOR), P(DP)),
        check_vma=False,
    )
```

```python
import functools

import jax
import jax.numpy as jnp
import numpy as np
from jax import lax
from jax.experimental import pallas as pl
from jax.experimental.pallas import tpu as pltpu
from jax.sharding import Mesh
from jax.sharding import PartitionSpec as P

tiny_square = 1e-30
decay_rate = 0.8
clip_level = 0.25
learn_rate = 0.01

FIRST = ("z_lo", "y_lo", "x")
SECOND = ("y_hi",)
DP = ("y_hi", "y_lo", "x", "z_lo")
TENSOR = ("z_hi", "core")
SIZES = (4, 2, 4, 2, 4, 2)
LANES = 128
MIB = 2**20

VMEM = pl.BlockSpec(memory_space=pltpu.VMEM)
SMEM = pl.BlockSpec(memory_space=pltpu.SMEM)


def product_kernel(chunk, act_hbm, cot_hbm, out_ref, act, cot, total, act_sems, cot_sems):
    tokens, cols = cot.shape
    members, block, _ = out_ref.shape
    owners, run = lax.axis_size(SECOND), block // lax.axis_size(SECOND)
    parts = [pl.ds(at, min(chunk, tokens - at)) for at in range(0, tokens, chunk)]
    copies = []
    for i, part in enumerate(parts):
        pair = (
            pltpu.make_async_copy(act_hbm.at[part], act.at[part], act_sems.at[i]),
            pltpu.make_async_copy(cot_hbm.at[part], cot.at[part], cot_sems.at[i]),
        )
        for copy in pair:
            copy.start()
        copies.append(pair)
    for i, part in enumerate(parts):
        for copy in copies[i]:
            copy.wait()
        value = jnp.dot(act[part].T, cot[part], preferred_element_type=jnp.float32)
        if i > 0:
            value = total[...] + value
        if i < len(parts) - 1:
            total[...] = value
    order = np.arange(members).reshape([lax.axis_size(name) for name in DP[1:]])
    order = order.transpose([DP[1:].index(name) for name in FIRST]).reshape(-1)
    for owner in range(owners):
        for member in range(members):
            at = (owner * members + int(order[member])) * run
            out_ref[member, owner * run : (owner + 1) * run, :] = value[at : at + run, :]


def product(activations, out_grad, members):
    tokens, rows = activations.shape
    cols = out_grad.shape[1]
    chunk = 512
    n = pl.cdiv(tokens, chunk)
    return pl.pallas_call(
        functools.partial(product_kernel, chunk),
        in_specs=[pl.BlockSpec(memory_space=pl.ANY)] * 2,
        out_specs=VMEM,
        out_shape=jax.ShapeDtypeStruct((members, rows // members, cols), jnp.float32),
        scratch_shapes=[
            pltpu.VMEM((tokens, rows), activations.dtype),
            pltpu.VMEM((tokens, cols), out_grad.dtype),
            pltpu.VMEM((rows, cols), jnp.float32),
            pltpu.SemaphoreType.DMA((n,)),
            pltpu.SemaphoreType.DMA((n,)),
        ],
        compiler_params=pltpu.CompilerParams(vmem_limit_bytes=56 * MIB),
        name="product",
    )(activations, out_grad)


def split_kernel(row_moment_ref, pieces_ref, out_ref):
    own, rows, cols = row_moment_ref.shape[1], pieces_ref.shape[1], pieces_ref.shape[2]
    members, place = out_ref.shape[0], lax.axis_index(SECOND)
    for c in range(cols // LANES):
        block = jnp.sum(pieces_ref[:, :, c * LANES : (c + 1) * LANES], axis=0)
        out_ref[:, c * rows : (c + 1) * rows, :] = jnp.broadcast_to(block[None], (members,) + block.shape)
    lane = lax.broadcasted_iota(jnp.int32, (8, LANES), 1)
    moments = jnp.zeros((8, LANES), jnp.float32)
    for r in range(own):
        moments = jnp.where(lane == place * own + r, row_moment_ref[:, r : r + 1], moments)
    out_ref[:, cols // LANES * rows :, :] = jnp.broadcast_to(moments[None], (members, 8, LANES))


def column_kernel(pieces_ref, grad_ref, moment_ref, copies_ref):
    rows, cols = grad_ref.shape
    for c in range(cols // LANES):
        at = slice(c * LANES, (c + 1) * LANES)
        grad = jnp.sum(pieces_ref[:, c * rows : (c + 1) * rows], axis=0)
        grad_ref[:, at] = grad
        sums = jnp.sum(grad * grad + tiny_square, axis=0, keepdims=True)
        copies_ref[:, :, at] = jnp.broadcast_to(sums[None], (copies_ref.shape[0], 1, LANES))
    moment_ref[...] = jnp.sum(pieces_ref[:, cols // LANES * rows :], axis=0)[:1]


def row_kernel(all_rows, all_cols, each, cols_ref, col_moment_ref, grad_ref, moment_ref, col_ref, message_ref):
    col_next = (
        decay_rate * col_moment_ref[...] + (1.0 - decay_rate) * jnp.sum(cols_ref[...], axis=0) / all_rows
    )
    col_ref[...] = col_next
    grad = grad_ref[...]
    rows, cols = grad.shape
    square = grad * grad
    both = jnp.concatenate([square + tiny_square, square / col_next], axis=0)
    both = sum(both[:, at : at + LANES] for at in range(0, cols, LANES))
    both = jnp.concatenate([both, jnp.zeros((LANES - 2 * rows, LANES), jnp.float32)], axis=0)
    sums = jnp.sum(both.T, axis=0, keepdims=True)
    sums = sums + (decay_rate / (1.0 - decay_rate) * all_cols / each) * moment_ref[...]
    message_ref[...] = jnp.broadcast_to(sums[None], message_ref.shape)


def to_lanes(column):
    n = column.shape[0]
    here = lax.broadcasted_iota(jnp.int32, (n, LANES), 0) == lax.broadcasted_iota(jnp.int32, (n, LANES), 1)
    return jnp.sum(jnp.where(here, jnp.broadcast_to(column, (n, LANES)), 0.0), axis=0)[:n]


def finish_kernel(
    all_rows, all_cols, message_ref, kept_ref, grad_ref, weight_ref, new_ref, step_ref, row_ref, col_ref, factor_ref
):
    place, member = lax.axis_index(SECOND), lax.axis_index(FIRST)
    own, rows = weight_ref.shape[0], grad_ref.shape[0]
    blocks = all_rows // rows
    each = message_ref.shape[0] // blocks
    sums = jnp.sum(message_ref[:, 0].reshape(blocks, each, LANES), axis=1)
    row_next = (1.0 - decay_rate) / all_cols * sums[:, :rows]
    scaled = sums[:, rows : 2 * rows] / row_next
    total = jnp.sum(jnp.sum(scaled, axis=1, keepdims=True), axis=0, keepdims=True)
    row_mean = jnp.sum(jnp.sum(row_next, axis=1, keepdims=True), axis=0, keepdims=True) / all_rows
    mine = lax.broadcasted_iota(jnp.int32, row_next.shape, 0) == member
    row_next = jnp.sum(jnp.where(mine, row_next, 0.0), axis=0, keepdims=True)
    lane = lax.broadcasted_iota(jnp.int32, (own, rows), 1)
    here = lax.broadcasted_iota(jnp.int32, (own, rows), 0) + place * own
    column = jnp.sum(jnp.where(lane == here, jnp.broadcast_to(row_next, (own, rows)), 0.0), axis=1, keepdims=True)
    row_ref[...] = to_lanes(column)
    factor_ref[...] = to_lanes(column / row_mean)
    rms = jnp.sqrt(total * row_mean / (all_rows * all_cols))
    grad = grad_ref[pl.ds(pl.multiple_of(place * own, own), own), :]
    col_next = kept_ref[...]
    col_ref[...] = col_next
    scaled = grad / jnp.sqrt(column * col_next / row_mean)
    step = scaled / jnp.maximum(1.0, rms / clip_level)
    step_ref[...] = step
    new_ref[...] = weight_ref[...] - learn_rate * step


def call(kernel, outs, ins, name):
    return pl.pallas_call(
        kernel,
        in_specs=ins,
        out_specs=[VMEM] * len(outs),
        out_shape=[jax.ShapeDtypeStruct(shape, jnp.float32) for shape in outs],
        compiler_params=pltpu.CompilerParams(vmem_limit_bytes=32 * MIB),
        name=name,
    )


def body(activations, out_grad, weight, row_moment, col_moment):
    own_rows, cols = weight.shape
    all_rows = own_rows * lax.axis_size(DP)
    all_cols = cols * lax.axis_size(TENSOR)
    first, second, tensor = lax.axis_size(FIRST), lax.axis_size(SECOND), lax.axis_size(TENSOR)
    rows = second * own_rows

    pieces = lax.all_to_all(product(activations, out_grad, first), FIRST, 0, 0)
    (pieces,) = call(split_kernel, [(second, rows * cols // LANES + 8, LANES)], [VMEM] * 2, "split")(
        row_moment.reshape(1, own_rows), pieces
    )
    pieces = lax.all_to_all(pieces, SECOND, 0, 0)
    grad, moment, copies = call(
        column_kernel, [(rows, cols), (1, LANES), (first, 1, cols)], [VMEM], "columns"
    )(pieces)
    copies = lax.all_to_all(copies, FIRST, 0, 0)
    kept, message = call(
        functools.partial(row_kernel, all_rows, all_cols, tensor),
        [(1, cols), (first * tensor, 1, LANES)],
        [VMEM] * 4,
        "rows",
    )(copies, col_moment.reshape(1, cols), grad, moment)
    message = lax.all_to_all(message, FIRST + TENSOR, 0, 0)
    new_weight, step_taken, row_next, col_next, row_factor = call(
        functools.partial(finish_kernel, all_rows, all_cols),
        [(own_rows, cols), (own_rows, cols), (own_rows,), (1, cols), (own_rows,)],
        [VMEM] * 4,
        "finish",
    )(message, kept, grad, weight)
    return new_weight, step_taken, row_next, col_next.reshape(cols), row_factor


def solution(mesh):
    physical = Mesh(mesh.devices.reshape(SIZES), DP + TENSOR)
    return jax.shard_map(
        body,
        mesh=physical,
        in_specs=(P(DP, None), P(DP, TENSOR), P(DP, TENSOR), P(DP), P(TENSOR)),
        out_specs=(P(DP, TENSOR), P(DP, TENSOR), P(DP), P(TENSOR), P(DP)),
        check_vma=False,
    )
```

```python
import functools
import math

import jax
import jax.numpy as jnp
import numpy as np
from jax import lax
from jax.experimental import pallas as pl
from jax.experimental.pallas import tpu as pltpu
from jax.sharding import Mesh
from jax.sharding import PartitionSpec as P

tiny_square = 1e-30
decay_rate = 0.8
clip_level = 0.25
learn_rate = 0.01

FIRST = ("z_lo", "y_lo", "x")
SECOND = ("y_hi",)
DP = ("y_hi", "y_lo", "x", "z_lo")
TENSOR = ("z_hi", "core")
SIZES = (4, 2, 4, 2, 4, 2)
LANES = 128
MIB = 2**20

VMEM = pl.BlockSpec(memory_space=pltpu.VMEM)
SMEM = pl.BlockSpec(memory_space=pltpu.SMEM)


def product_kernel(chunk, width, act_hbm, cot_hbm, out_hbm, act, cot, total, out, act_sems, cot_sems, out_sems):
    tokens, cols = cot.shape
    members, block, _ = out.shape
    owners, run = lax.axis_size(SECOND), block // lax.axis_size(SECOND)
    order = np.arange(members).reshape([lax.axis_size(name) for name in DP[1:]])
    order = order.transpose([DP[1:].index(name) for name in FIRST]).reshape(-1)
    parts = [pl.ds(at, min(chunk, tokens - at)) for at in range(0, tokens, chunk)]
    copies = []
    for i, part in enumerate(parts):
        pair = (
            pltpu.make_async_copy(act_hbm.at[part], act.at[part], act_sems.at[i]),
            pltpu.make_async_copy(cot_hbm.at[part], cot.at[part], cot_sems.at[i]),
        )
        for copy in pair:
            copy.start()
        copies.append(pair)
    for i, part in enumerate(parts[:-1]):
        for copy in copies[i]:
            copy.wait()
        value = jnp.dot(act[part].T, cot[part], preferred_element_type=jnp.float32)
        total[...] = value if i == 0 else total[...] + value
    for copy in copies[-1]:
        copy.wait()
    left = act[parts[-1]].T
    results = []
    for j, at in enumerate(range(0, cols, width)):
        here = slice(at, at + width)
        value = total[:, here] + jnp.dot(left, cot[parts[-1], here], preferred_element_type=jnp.float32)
        for owner in range(owners):
            for member in range(members):
                row = (owner * members + int(order[member])) * run
                out[member, owner * run : (owner + 1) * run, here] = value[row : row + run, :]
        columns = pl.ds(at, width)
        copy = pltpu.make_async_copy(out.at[:, :, columns], out_hbm.at[:, :, columns], out_sems.at[j])
        copy.start()
        results.append(copy)
    for copy in results:
        copy.wait()


def product(activations, out_grad, members):
    tokens, rows = activations.shape
    cols = out_grad.shape[1]
    chunk, width = 512, 256
    n = pl.cdiv(tokens, chunk)
    shape = (members, rows // members, cols)
    return pl.pallas_call(
        functools.partial(product_kernel, chunk, width),
        in_specs=[pl.BlockSpec(memory_space=pl.ANY)] * 2,
        out_specs=pl.BlockSpec(memory_space=pl.ANY),
        out_shape=jax.ShapeDtypeStruct(shape, jnp.float32),
        scratch_shapes=[
            pltpu.VMEM((tokens, rows), activations.dtype),
            pltpu.VMEM((tokens, cols), out_grad.dtype),
            pltpu.VMEM((rows, cols), jnp.float32),
            pltpu.VMEM(shape, jnp.float32),
            pltpu.SemaphoreType.DMA((n,)),
            pltpu.SemaphoreType.DMA((n,)),
            pltpu.SemaphoreType.DMA((cols // width,)),
        ],
        compiler_params=pltpu.CompilerParams(vmem_limit_bytes=56 * MIB),
        name="product",
    )(activations, out_grad)


def split_kernel(row_moment_ref, pieces_ref, out_ref):
    own, rows, cols = row_moment_ref.shape[1], pieces_ref.shape[1], pieces_ref.shape[2]
    members, place = out_ref.shape[0], lax.axis_index(SECOND)
    for c in range(cols // LANES):
        block = jnp.sum(pieces_ref[:, :, c * LANES : (c + 1) * LANES], axis=0)
        out_ref[:, c * rows : (c + 1) * rows, :] = jnp.broadcast_to(block[None], (members,) + block.shape)
    lane = lax.broadcasted_iota(jnp.int32, (8, LANES), 1)
    moments = jnp.zeros((8, LANES), jnp.float32)
    for r in range(own):
        moments = jnp.where(lane == place * own + r, row_moment_ref[:, r : r + 1], moments)
    out_ref[:, cols // LANES * rows :, :] = jnp.broadcast_to(moments[None], (members, 8, LANES))


def column_kernel(pieces_ref, grad_ref, moment_ref, copies_ref):
    rows, cols = grad_ref.shape
    for c in range(cols // LANES):
        at = slice(c * LANES, (c + 1) * LANES)
        grad = jnp.sum(pieces_ref[:, c * rows : (c + 1) * rows], axis=0)
        grad_ref[:, at] = grad
        sums = jnp.sum(grad * grad + tiny_square, axis=0, keepdims=True)
        copies_ref[:, :, at] = jnp.broadcast_to(sums[None], (copies_ref.shape[0], 1, LANES))
    moment_ref[...] = jnp.sum(pieces_ref[:, cols // LANES * rows :], axis=0)[:1]


def row_kernel(all_rows, all_cols, each, cols_ref, col_moment_ref, grad_ref, moment_ref, col_ref, message_ref):
    col_next = (
        decay_rate * col_moment_ref[...] + (1.0 - decay_rate) * jnp.sum(cols_ref[...], axis=0) / all_rows
    )
    col_ref[...] = col_next
    grad = grad_ref[...]
    rows, cols = grad.shape
    square = grad * grad
    both = jnp.concatenate([square + tiny_square, square / col_next], axis=0)
    both = sum(both[:, at : at + LANES] for at in range(0, cols, LANES))
    both = jnp.concatenate([both, jnp.zeros((LANES - 2 * rows, LANES), jnp.float32)], axis=0)
    sums = jnp.sum(both.T, axis=0, keepdims=True)
    sums = sums + (decay_rate / (1.0 - decay_rate) * all_cols / each) * moment_ref[...]
    message_ref[...] = jnp.broadcast_to(sums[None], message_ref.shape)


def to_lanes(column):
    n = column.shape[0]
    here = lax.broadcasted_iota(jnp.int32, (n, LANES), 0) == lax.broadcasted_iota(jnp.int32, (n, LANES), 1)
    return jnp.sum(jnp.where(here, jnp.broadcast_to(column, (n, LANES)), 0.0), axis=0)[:n]


def finish_kernel(
    all_rows, all_cols, message_ref, kept_ref, grad_ref, weight_ref, new_ref, step_ref, row_ref, col_ref, factor_ref
):
    place, member = lax.axis_index(SECOND), lax.axis_index(FIRST)
    own, rows = weight_ref.shape[0], grad_ref.shape[0]
    blocks = all_rows // rows
    each = message_ref.shape[0] // blocks
    sums = jnp.sum(message_ref[:, 0].reshape(blocks, each, LANES), axis=1)
    row_next = (1.0 - decay_rate) / all_cols * sums[:, :rows]
    scaled = sums[:, rows : 2 * rows] / row_next
    total = jnp.sum(jnp.sum(scaled, axis=1, keepdims=True), axis=0, keepdims=True)
    row_mean = jnp.sum(jnp.sum(row_next, axis=1, keepdims=True), axis=0, keepdims=True) / all_rows
    mine = lax.broadcasted_iota(jnp.int32, row_next.shape, 0) == member
    row_next = jnp.sum(jnp.where(mine, row_next, 0.0), axis=0, keepdims=True)
    lane = lax.broadcasted_iota(jnp.int32, (own, rows), 1)
    here = lax.broadcasted_iota(jnp.int32, (own, rows), 0) + place * own
    column = jnp.sum(jnp.where(lane == here, jnp.broadcast_to(row_next, (own, rows)), 0.0), axis=1, keepdims=True)
    row_ref[...] = to_lanes(column)
    factor_ref[...] = to_lanes(column / row_mean)
    rms = jnp.sqrt(total * row_mean / (all_rows * all_cols))
    grad = grad_ref[pl.ds(pl.multiple_of(place * own, own), own), :]
    col_next = kept_ref[...]
    col_ref[...] = col_next
    scaled = grad / jnp.sqrt(column * col_next / row_mean)
    step = scaled / jnp.maximum(1.0, rms / clip_level)
    step_ref[...] = step
    new_ref[...] = weight_ref[...] - learn_rate * step


def call(kernel, outs, ins, name):
    return pl.pallas_call(
        kernel,
        in_specs=ins,
        out_specs=[VMEM] * len(outs),
        out_shape=[jax.ShapeDtypeStruct(shape, jnp.float32) for shape in outs],
        compiler_params=pltpu.CompilerParams(vmem_limit_bytes=32 * MIB),
        name=name,
    )


def body(activations, out_grad, weight, row_moment, col_moment):
    own_rows, cols = weight.shape
    all_rows = own_rows * lax.axis_size(DP)
    all_cols = cols * lax.axis_size(TENSOR)
    first, second, tensor = lax.axis_size(FIRST), lax.axis_size(SECOND), lax.axis_size(TENSOR)
    rows = second * own_rows

    pieces = lax.all_to_all(product(activations, out_grad, first), FIRST, 0, 0)
    (pieces,) = call(split_kernel, [(second, rows * cols // LANES + 8, LANES)], [VMEM] * 2, "split")(
        row_moment.reshape(1, own_rows), pieces
    )
    places = np.arange(math.prod(SIZES)).reshape(second, -1, SIZES[-1])
    groups = [[int(d) for d in places[:: 1 - 2 * core, i, core]] for i in range(places.shape[1]) for core in range(SIZES[-1])]
    pieces = lax.all_to_all(pieces, DP + TENSOR, 0, 0, axis_index_groups=groups)
    grad, moment, copies = call(
        column_kernel, [(rows, cols), (1, LANES), (first, 1, cols)], [VMEM], "columns"
    )(pieces)
    copies = lax.all_to_all(copies, FIRST, 0, 0)
    kept, message = call(
        functools.partial(row_kernel, all_rows, all_cols, tensor),
        [(1, cols), (first * tensor, 1, LANES)],
        [VMEM] * 4,
        "rows",
    )(copies, col_moment.reshape(1, cols), grad, moment)
    message = lax.all_to_all(message, FIRST + TENSOR, 0, 0)
    new_weight, step_taken, row_next, col_next, row_factor = call(
        functools.partial(finish_kernel, all_rows, all_cols),
        [(own_rows, cols), (own_rows, cols), (own_rows,), (1, cols), (own_rows,)],
        [VMEM] * 4,
        "finish",
    )(message, kept, grad, weight)
    return new_weight, step_taken, row_next, col_next.reshape(cols), row_factor


def solution(mesh):
    physical = Mesh(mesh.devices.reshape(SIZES), DP + TENSOR)
    return jax.shard_map(
        body,
        mesh=physical,
        in_specs=(P(DP, None), P(DP, TENSOR), P(DP, TENSOR), P(DP), P(TENSOR)),
        out_specs=(P(DP, TENSOR), P(DP, TENSOR), P(DP), P(TENSOR), P(DP)),
        check_vma=False,
    )
```

```python
import functools
import math

import jax
import jax.numpy as jnp
import numpy as np
from jax import lax
from jax.experimental import pallas as pl
from jax.experimental.pallas import tpu as pltpu
from jax.sharding import Mesh
from jax.sharding import PartitionSpec as P

tiny_square = 1e-30
decay_rate = 0.8
clip_level = 0.25
learn_rate = 0.01

FIRST = ("z_lo", "y_lo", "x")
SECOND = ("y_hi",)
DP = ("y_hi", "y_lo", "x", "z_lo")
TENSOR = ("z_hi", "core")
SIZES = (4, 2, 4, 2, 4, 2)
LANES = 128
MIB = 2**20

VMEM = pl.BlockSpec(memory_space=pltpu.VMEM)
SMEM = pl.BlockSpec(memory_space=pltpu.SMEM)


def product_kernel(chunk, width, act_hbm, cot_hbm, out_hbm, act, cot, total, out, act_sems, cot_sems, out_sems):
    tokens, cols = cot.shape
    members, block, _ = out.shape
    owners, run = lax.axis_size(SECOND), block // lax.axis_size(SECOND)
    order = np.arange(members).reshape([lax.axis_size(name) for name in DP[1:]])
    order = order.transpose([DP[1:].index(name) for name in FIRST]).reshape(-1)
    parts = [pl.ds(at, min(chunk, tokens - at)) for at in range(0, tokens, chunk)]
    copies = []
    for i, part in enumerate(parts):
        pair = (
            pltpu.make_async_copy(act_hbm.at[part], act.at[part], act_sems.at[i]),
            pltpu.make_async_copy(cot_hbm.at[part], cot.at[part], cot_sems.at[i]),
        )
        for copy in pair:
            copy.start()
        copies.append(pair)
    for i, part in enumerate(parts[:-1]):
        for copy in copies[i]:
            copy.wait()
        value = jnp.dot(act[part].T, cot[part], preferred_element_type=jnp.float32)
        total[...] = value if i == 0 else total[...] + value
    for copy in copies[-1]:
        copy.wait()
    left = act[parts[-1]].T
    results = []
    for j, at in enumerate(range(0, cols, width)):
        here = slice(at, at + width)
        value = total[:, here] + jnp.dot(left, cot[parts[-1], here], preferred_element_type=jnp.float32)
        for owner in range(owners):
            for member in range(members):
                row = (owner * members + int(order[member])) * run
                out[member, owner * run : (owner + 1) * run, here] = value[row : row + run, :]
        columns = pl.ds(at, width)
        copy = pltpu.make_async_copy(out.at[:, :, columns], out_hbm.at[:, :, columns], out_sems.at[j])
        copy.start()
        results.append(copy)
    for copy in results:
        copy.wait()


def product(activations, out_grad, members):
    tokens, rows = activations.shape
    cols = out_grad.shape[1]
    chunk, width = 512, 256
    n = pl.cdiv(tokens, chunk)
    shape = (members, rows // members, cols)
    return pl.pallas_call(
        functools.partial(product_kernel, chunk, width),
        in_specs=[pl.BlockSpec(memory_space=pl.ANY)] * 2,
        out_specs=pl.BlockSpec(memory_space=pl.ANY),
        out_shape=jax.ShapeDtypeStruct(shape, jnp.float32),
        scratch_shapes=[
            pltpu.VMEM((tokens, rows), activations.dtype),
            pltpu.VMEM((tokens, cols), out_grad.dtype),
            pltpu.VMEM((rows, cols), jnp.float32),
            pltpu.VMEM(shape, jnp.float32),
            pltpu.SemaphoreType.DMA((n,)),
            pltpu.SemaphoreType.DMA((n,)),
            pltpu.SemaphoreType.DMA((cols // width,)),
        ],
        compiler_params=pltpu.CompilerParams(vmem_limit_bytes=56 * MIB),
        name="product",
    )(activations, out_grad)


def split_kernel(row_moment_ref, pieces_ref, out_ref):
    own, rows, cols = row_moment_ref.shape[1], pieces_ref.shape[1], pieces_ref.shape[2]
    members, place = out_ref.shape[0], lax.axis_index(SECOND)
    for c in range(cols // LANES):
        block = jnp.sum(pieces_ref[:, :, c * LANES : (c + 1) * LANES], axis=0)
        out_ref[:, c * rows : (c + 1) * rows, :] = jnp.broadcast_to(block[None], (members,) + block.shape)
    lane = lax.broadcasted_iota(jnp.int32, (8, LANES), 1)
    moments = jnp.zeros((8, LANES), jnp.float32)
    for r in range(own):
        moments = jnp.where(lane == place * own + r, row_moment_ref[:, r : r + 1], moments)
    out_ref[:, cols // LANES * rows :, :] = jnp.broadcast_to(moments[None], (members, 8, LANES))


def column_kernel(pieces_ref, grad_ref, moment_ref, copies_ref):
    rows, cols = grad_ref.shape
    for c in range(cols // LANES):
        at = slice(c * LANES, (c + 1) * LANES)
        grad = jnp.sum(pieces_ref[:, c * rows : (c + 1) * rows], axis=0)
        grad_ref[:, at] = grad
        sums = jnp.sum(grad * grad + tiny_square, axis=0, keepdims=True)
        copies_ref[:, :, at] = jnp.broadcast_to(sums[None], (copies_ref.shape[0], 1, LANES))
    moment_ref[...] = jnp.sum(pieces_ref[:, cols // LANES * rows :], axis=0)[:1]


def row_kernel(all_rows, all_cols, each, cols_ref, col_moment_ref, grad_ref, moment_ref, col_ref, message_ref):
    col_next = (
        decay_rate * col_moment_ref[...] + (1.0 - decay_rate) * jnp.sum(cols_ref[...], axis=0) / all_rows
    )
    col_ref[...] = col_next
    grad = grad_ref[...]
    rows, cols = grad.shape
    square = grad * grad
    both = jnp.concatenate([square + tiny_square, square / col_next], axis=0)
    both = sum(both[:, at : at + LANES] for at in range(0, cols, LANES))
    both = jnp.concatenate([both, jnp.zeros((LANES - 2 * rows, LANES), jnp.float32)], axis=0)
    sums = jnp.sum(both.T, axis=0, keepdims=True)
    sums = sums + (decay_rate / (1.0 - decay_rate) * all_cols / each) * moment_ref[...]
    message_ref[...] = jnp.broadcast_to(sums[None], message_ref.shape)


def to_lanes(column):
    n = column.shape[0]
    here = lax.broadcasted_iota(jnp.int32, (n, LANES), 0) == lax.broadcasted_iota(jnp.int32, (n, LANES), 1)
    return jnp.sum(jnp.where(here, jnp.broadcast_to(column, (n, LANES)), 0.0), axis=0)[:n]


def finish_kernel(
    all_rows, all_cols, message_ref, kept_ref, grad_ref, weight_ref, new_ref, step_ref, row_ref, col_ref, factor_ref
):
    place, member = lax.axis_index(SECOND), lax.axis_index(FIRST)
    own, rows = weight_ref.shape[0], grad_ref.shape[0]
    blocks = all_rows // rows
    each = message_ref.shape[0] // blocks
    sums = jnp.sum(message_ref[:, 0].reshape(blocks, each, LANES), axis=1)
    row_next = (1.0 - decay_rate) / all_cols * sums[:, :rows]
    scaled = sums[:, rows : 2 * rows] / row_next
    total = jnp.sum(jnp.sum(scaled, axis=1, keepdims=True), axis=0, keepdims=True)
    row_mean = jnp.sum(jnp.sum(row_next, axis=1, keepdims=True), axis=0, keepdims=True) / all_rows
    mine = lax.broadcasted_iota(jnp.int32, row_next.shape, 0) == member
    row_next = jnp.sum(jnp.where(mine, row_next, 0.0), axis=0, keepdims=True)
    lane = lax.broadcasted_iota(jnp.int32, (own, rows), 1)
    here = lax.broadcasted_iota(jnp.int32, (own, rows), 0) + place * own
    column = jnp.sum(jnp.where(lane == here, jnp.broadcast_to(row_next, (own, rows)), 0.0), axis=1, keepdims=True)
    row_ref[...] = to_lanes(column)
    factor_ref[...] = to_lanes(column / row_mean)
    rms = jnp.sqrt(total * row_mean / (all_rows * all_cols))
    grad = grad_ref[pl.ds(pl.multiple_of(place * own, own), own), :]
    col_next = kept_ref[...]
    col_ref[...] = col_next
    scaled = grad / jnp.sqrt(column * col_next / row_mean)
    step = scaled / jnp.maximum(1.0, rms / clip_level)
    step_ref[...] = step
    new_ref[...] = weight_ref[...] - learn_rate * step


def call(kernel, outs, ins, name):
    return pl.pallas_call(
        kernel,
        in_specs=ins,
        out_specs=[VMEM] * len(outs),
        out_shape=[jax.ShapeDtypeStruct(shape, jnp.float32) for shape in outs],
        compiler_params=pltpu.CompilerParams(vmem_limit_bytes=32 * MIB),
        name=name,
    )


def body(activations, out_grad, weight, row_moment, col_moment):
    own_rows, cols = weight.shape
    all_rows = own_rows * lax.axis_size(DP)
    all_cols = cols * lax.axis_size(TENSOR)
    first, second, tensor = lax.axis_size(FIRST), lax.axis_size(SECOND), lax.axis_size(TENSOR)
    rows = second * own_rows

    pieces = lax.all_to_all(product(activations, out_grad, first), FIRST, 0, 0)
    (pieces,) = call(split_kernel, [(second, rows * cols // LANES + 8, LANES)], [VMEM] * 2, "split")(
        row_moment.reshape(1, own_rows), pieces
    )
    places = np.arange(math.prod(SIZES)).reshape(second, -1, SIZES[-1])
    groups = [[int(d) for d in places[:: 1 - 2 * core, i, core]] for i in range(places.shape[1]) for core in range(SIZES[-1])]
    pieces = lax.all_to_all(pieces, DP + TENSOR, 0, 0, axis_index_groups=groups)
    grad, moment, copies = call(
        column_kernel, [(rows, cols), (1, LANES), (first, 1, cols)], [VMEM], "columns"
    )(pieces)
    places = np.arange(math.prod(SIZES)).reshape(second, first, -1, SIZES[-1])
    groups = [
        [int(d) for d in places[i, :: 1 - 2 * core, j, core]]
        for i in range(second)
        for j in range(places.shape[2])
        for core in range(SIZES[-1])
    ]
    copies = lax.all_to_all(copies, DP + TENSOR, 0, 0, axis_index_groups=groups)
    kept, message = call(
        functools.partial(row_kernel, all_rows, all_cols, tensor),
        [(1, cols), (first * tensor, 1, LANES)],
        [VMEM] * 4,
        "rows",
    )(copies, col_moment.reshape(1, cols), grad, moment)
    message = lax.all_to_all(message, FIRST + TENSOR, 0, 0)
    new_weight, step_taken, row_next, col_next, row_factor = call(
        functools.partial(finish_kernel, all_rows, all_cols),
        [(own_rows, cols), (own_rows, cols), (own_rows,), (1, cols), (own_rows,)],
        [VMEM] * 4,
        "finish",
    )(message, kept, grad, weight)
    return new_weight, step_taken, row_next, col_next.reshape(cols), row_factor


def solution(mesh):
    physical = Mesh(mesh.devices.reshape(SIZES), DP + TENSOR)
    return jax.shard_map(
        body,
        mesh=physical,
        in_specs=(P(DP, None), P(DP, TENSOR), P(DP, TENSOR), P(DP), P(TENSOR)),
        out_specs=(P(DP, TENSOR), P(DP, TENSOR), P(DP), P(TENSOR), P(DP)),
        check_vma=False,
    )
```
